32 devices in a mesh: groups: 2 (over y), tm: 4 (over z), chan: 2 (over x), sub: 2 (over core).
Axes of the slice: x: 2, y: 2, z: 4, core: 2. Of those that a mesh axis runs over, the one named last changes fastest.
Arguments:
- signal: bfloat16 [2, 240, 65536], P(None, 'chan', ('groups', 'tm', 'sub')), parts along dimension 2, may hold values from -6 to 6
- channel_mask: int32 [240], P('chan'), may hold values from 0 to 1, as said below
- dispersion: float32 [240], P('chan'), may hold values from 1228.8 to 12288
- equaliser: bfloat16 [96, 2, 240, 240], P(('tm', 'chan')), may hold values from -0.25 to 0.25
- bin_block: int32 [64, 128], P(None, ('tm', 'chan')), may hold values from 0 to 11
Outputs:
- output: bfloat16 [2, 240, 65536], P(None, 'chan', ('groups', 'tm', 'sub')), parts along dimension 2
The draws below stay inside these ranges and needn't reach their ends.
There are 2 independent parts, one for each index of `groups`. The reference program is written for one: setup_inputs(seed, part) draws one part's arguments, and reference() takes and returns one part's arrays. A program takes and returns all parts, laid end to end along the dimension named above; an argument that names none is the same for every part. Nothing has to cross between parts.
Inputs may be any that keep to these rules, and one draw needn't show every extreme that they name: `channel_mask`: exactly 228 entries are 1.
All inputs are finite; a program needn't handle non-finite values.
Results may differ from the reference program's by a relative error of at most 0.0089.
Values may be sent and summed in bfloat16 or wider, within the bound.
A program may use at most 128 MiB of HBM per device.

```python
import math
import jax
import jax.numpy as jnp
from jax import lax

C = 240
VALID = 228
TAPS = 4096
N1 = 128
NB_DEV = 12
NFFT = 8192
N2 = 64
KD = 16
NBLK = 96
TIME = 32768


def draw_channel_mask(key, part):
    order = jax.random.permutation(key, C)
    return jnp.where(order >= C - VALID, 1, 0).astype(jnp.int32)


def set_ends(values, rng, low, high):
    dims = values.shape
    place = [jax.random.randint(jax.random.fold_in(rng, axis), (), 0, dims[axis]) for axis in range(len(dims))]
    values = values.at[tuple(place)].set(low)
    longest = dims.index(max(dims))
    place[longest] = (place[longest] + 1) % dims[longest]
    return values.at[tuple(place)].set(high)


def block_scale(own_key, dims, cuts, low, largest):
    gain, own = 1.0, jax.random.fold_in(own_key, 6)
    for axis_at, shards_of in cuts:
        heights = jnp.exp(jax.random.uniform(jax.random.fold_in(own, axis_at), (shards_of,), jnp.float32, low / len(cuts), largest / len(cuts)))
        gain = gain * jnp.repeat(heights, dims[axis_at] // shards_of).reshape([-1 if axis == axis_at else 1 for axis in range(len(dims))])
    return gain


def gaussian(key, shape, width, limit, pieces=(), held_as=jnp.bfloat16):
    drawn = jax.random.normal(key, shape, jnp.float32) * width
    if len(pieces) > 0:
        drawn = block_scale(key, shape, pieces, -0.22, 0.18) * drawn
    return jnp.clip(drawn, min=-limit, max=limit).astype(held_as)


def setup_inputs(seed: int = 0, part: int = 0) -> dict:
    keys = jax.random.split(jax.random.key(seed), 6)
    part_keys = jax.random.split(jax.random.fold_in(keys[5], part), 6)
    signal = gaussian(part_keys[0], (2, C, TIME), 1.0, 6.0, ((1, 2), (2, 8)))
    channel_mask = draw_channel_mask(jax.random.fold_in(keys[5], 71), part)
    dispersion = jnp.clip(1228.8 + 11059.2 * jax.random.uniform(keys[2], (C,), jnp.float32) ** block_scale(keys[2], (C,), ((0, 2),), -0.2, 0.2), 1228.8, 12288.0)
    equaliser = gaussian(keys[3], (NBLK, 2, C, C), (2 * C) ** -0.5, 0.25, ((0, 8),))
    bin_block = set_ends(jax.random.randint(keys[4], (N2, N1), 0, NB_DEV), jax.random.fold_in(keys[4], 1), 0, NB_DEV - 1).astype(jnp.int32)
    return {"signal": signal, "channel_mask": channel_mask, "dispersion": dispersion, "equaliser": equaliser, "bin_block": bin_block}


def dft_table(length, inverse):
    counter = jnp.arange(length, dtype=jnp.int32)
    product = counter[:, None] * counter[None, :] % length
    angle = product.astype(jnp.float32) * (2.0 * math.pi / length)
    factor = 1.0 / math.sqrt(length)
    cosine = jnp.cos(angle) * factor
    sine = jnp.sin(angle) * factor
    if inverse:
        upper = jnp.stack([cosine, -sine], axis=1)
        lower = jnp.stack([sine, cosine], axis=1)
    else:
        upper = jnp.stack([cosine, sine], axis=1)
        lower = jnp.stack([-sine, cosine], axis=1)
    return jnp.stack([upper, lower], axis=0).astype(jnp.bfloat16)

def twist_table(first_rows, columns):
    seconds = jnp.arange(columns, dtype=jnp.int32)
    product = first_rows[:, None] * seconds[None, :] % NFFT
    angle = product.astype(jnp.float32) * (2.0 * math.pi / NFFT)
    return (jnp.cos(angle), jnp.sin(angle))

def phase_table(dispersion):
    first_rows = jnp.arange(N1, dtype=jnp.int32)
    seconds = jnp.arange(N2, dtype=jnp.int32)
    bins = first_rows[:, None] + N1 * seconds[None, :]
    centred = jnp.where(bins < NFFT // 2, bins, bins - NFFT)
    freq_sq = (centred * centred).astype(jnp.float32) / float(NFFT * NFFT)
    quarter = jnp.mod(centred, 4).astype(jnp.float32) * (0.5 * math.pi)
    phase = dispersion[:, None, None] * freq_sq[None] - quarter[None]
    return (jnp.cos(phase), jnp.sin(phase))

def reference(signal, channel_mask, dispersion, equaliser, bin_block):
    mask_half = channel_mask.astype(jnp.bfloat16)
    masked = signal * mask_half[None, :, None]
    frame_count = TIME // TAPS
    padded = jnp.concatenate([jnp.zeros((2, C, TAPS), jnp.bfloat16), masked], axis=2)
    halves = padded.reshape(2, C, frame_count + 1, TAPS)
    frames = jnp.concatenate([halves[:, :, :-1], halves[:, :, 1:]], axis=3)
    forward_first = dft_table(N1, False).astype(jnp.float32)
    forward_second = dft_table(N2, False).astype(jnp.float32)
    inverse_first = dft_table(N1, True).astype(jnp.float32)
    inverse_second = dft_table(N2, True).astype(jnp.float32)
    cos_twist, sin_twist = twist_table(jnp.arange(N1, dtype=jnp.int32), N2)
    cos_disp, sin_disp = phase_table(dispersion)

    def forward(frame):
        shaped = frame.reshape(2, C, N1, N2).astype(jnp.float32)
        section_a = jnp.einsum('pkqt,qcts->cpks', forward_first, shaped)
        real_a = section_a[:, 0]
        imag_a = section_a[:, 1]
        twisted = jnp.stack([real_a * cos_twist + imag_a * sin_twist, imag_a * cos_twist - real_a * sin_twist], axis=1).astype(jnp.bfloat16)
        spectrum = jnp.einsum('rlps,cpks->ckrl', forward_second, twisted.astype(jnp.float32))
        real_s = spectrum[:, :, 0]
        imag_s = spectrum[:, :, 1]
        dispersed = jnp.stack([real_s * cos_disp - imag_s * sin_disp, real_s * sin_disp + imag_s * cos_disp], axis=2)
        return dispersed.astype(jnp.bfloat16)
    spectra = lax.map(forward, jnp.moveaxis(frames, 2, 0))
    groups_of = jnp.arange(N1, dtype=jnp.int32) // KD * NB_DEV
    blocks = groups_of[None, :] + bin_block

    def equalise(inputs):
        columns, picks = inputs
        chosen = jnp.take(equaliser, picks, axis=0).astype(jnp.float32)
        mixed = jnp.einsum('jsoc,mcjq->mojsq', chosen, columns.astype(jnp.float32))
        real_e = mixed[..., 0, 0] - mixed[..., 1, 1]
        imag_e = mixed[..., 0, 1] + mixed[..., 1, 0]
        return jnp.stack([real_e, imag_e], axis=-1).astype(jnp.bfloat16)
    equalised = lax.map(equalise, (jnp.moveaxis(spectra, 4, 0), blocks))
    equalised = jnp.transpose(equalised, (1, 2, 3, 4, 0))

    def inverse(spectrum):
        partial_value = jnp.einsum('rtpk,cjpk->crjt', inverse_second, spectrum.astype(jnp.float32))
        real_g = partial_value[:, 0]
        imag_g = partial_value[:, 1]
        turned = jnp.stack([real_g * cos_twist - imag_g * sin_twist, imag_g * cos_twist + real_g * sin_twist], axis=1).astype(jnp.bfloat16)
        values = jnp.einsum('rupj,cpjt->rcut', inverse_first[:, N1 // 2:], turned.astype(jnp.float32))
        return values.reshape(2, C, TAPS)
    outputs = lax.map(inverse, equalised)
    result = jnp.moveaxis(outputs, 0, 2).reshape(2, C, TIME)
    return (result * channel_mask.astype(jnp.float32)[None, :, None]).astype(jnp.bfloat16)
```

```python
import math

import jax
import jax.numpy as jnp
from jax import lax
from jax.experimental import pallas as pl
from jax.experimental.pallas import tpu as pltpu
from jax.sharding import PartitionSpec as P

TAPS = 4096
N1 = 128
NFFT = 8192
N2 = 64


def from_behind(value, axis, by):
    devices = lax.axis_size(axis)
    pairs = [(i, i + by) for i in range(devices) if 0 <= i + by < devices]
    return lax.ppermute(value, axis, pairs)


def dft_table(length, inverse):
    counter = jnp.arange(length, dtype=jnp.int32)
    product = counter[:, None] * counter[None, :] % length
    angle = product.astype(jnp.float32) * (2.0 * math.pi / length)
    factor = 1.0 / math.sqrt(length)
    cosine = jnp.cos(angle) * factor
    sine = jnp.sin(angle) * factor
    if inverse:
        upper = jnp.stack([cosine, -sine], axis=1)
        lower = jnp.stack([sine, cosine], axis=1)
    else:
        upper = jnp.stack([cosine, sine], axis=1)
        lower = jnp.stack([-sine, cosine], axis=1)
    return jnp.stack([upper, lower], axis=0).astype(jnp.bfloat16)


def twist_table(first_rows, columns):
    seconds = jnp.arange(columns, dtype=jnp.int32)
    product = first_rows[:, None] * seconds[None, :] % NFFT
    angle = product.astype(jnp.float32) * (2.0 * math.pi / NFFT)
    return (jnp.cos(angle), jnp.sin(angle))


def phase_table(dispersion):
    first_rows = jnp.arange(N1, dtype=jnp.int32)
    seconds = jnp.arange(N2, dtype=jnp.int32)
    bins = first_rows[:, None] + N1 * seconds[None, :]
    centred = jnp.where(bins < NFFT // 2, bins, bins - NFFT)
    freq_sq = (centred * centred).astype(jnp.float32) / float(NFFT * NFFT)
    quarter = jnp.mod(centred, 4).astype(jnp.float32) * (0.5 * math.pi)
    phase = dispersion[:, None, None] * freq_sq[None] - quarter[None]
    return (jnp.cos(phase), jnp.sin(phase))


def invert_second(spectra, first_rows, inverse_second):
    partial_value = jnp.einsum(
        "rspk,jfcpk->cjfrs", inverse_second, spectra, preferred_element_type=jnp.float32
    )
    cos_inv, sin_inv = twist_table(first_rows, N2)
    cos_inv = cos_inv[:, None, :]
    sin_inv = sin_inv[:, None, :]
    real_g = partial_value[:, :, :, 0]
    imag_g = partial_value[:, :, :, 1]
    turned = jnp.stack(
        [real_g * cos_inv - imag_g * sin_inv, imag_g * cos_inv + real_g * sin_inv], axis=3
    )
    return turned.astype(jnp.bfloat16)


def equalise_kernel(picks_ref, weights_ref, columns_ref, out_ref):
    values = columns_ref[0].astype(jnp.float32)
    channels, width = values.shape
    chosen = jnp.broadcast_to(picks_ref[...], values.shape)
    mixed = jnp.zeros((2 * channels, width), jnp.float32)
    for block in range(weights_ref.shape[0]):
        part = jnp.where(chosen == block, values, 0.0).astype(jnp.bfloat16)
        mixed = mixed + jnp.dot(
            weights_ref[block], part, preferred_element_type=jnp.float32
        )
    lane = lax.broadcasted_iota(jnp.int32, (channels, 2 * N2), 1)
    for start in range(0, width, 2 * N2):
        by_real = mixed[:channels, start : start + 2 * N2]
        by_imag = pltpu.roll(mixed[channels:, start : start + 2 * N2], N2, 1)
        turned = by_real + jnp.where(lane < N2, -by_imag, by_imag)
        out_ref[0, :, start : start + 2 * N2] = turned.astype(jnp.bfloat16)


def equalise(columns, equaliser, picks):
    frames, channels, lanes = columns.shape
    blocks = equaliser.shape[0]
    width = math.gcd(lanes, 8 * N2)
    weights = equaliser.reshape(blocks, 2 * channels, channels)
    spec = pl.BlockSpec((1, channels, width), lambda m, i: (m, 0, i))
    return pl.pallas_call(
        equalise_kernel,
        grid=(frames, lanes // width),
        in_specs=[
            pl.BlockSpec((1, width), lambda m, i: (0, i)),
            pl.BlockSpec((blocks, 2 * channels, channels), lambda m, i: (0, 0, 0)),
            spec,
        ],
        out_specs=spec,
        out_shape=jax.ShapeDtypeStruct(columns.shape, jnp.bfloat16),
        compiler_params=pltpu.CompilerParams(vmem_limit_bytes=40 * 1024 * 1024),
    )(picks, weights, columns)


def on_device(signal, channel_mask, dispersion, equaliser, bin_block):
    channels_dev = signal.shape[1]
    frame_count = signal.shape[2] // TAPS
    half_rows = N1 // 2
    mask_half = channel_mask.astype(jnp.bfloat16)
    masked = signal * mask_half[None, :, None]
    tail_in = from_behind(masked, ("tm", "sub"), 1)
    forward_first = dft_table(N1, False)
    forward_second = dft_table(N2, False)
    inverse_first = dft_table(N1, True)
    inverse_second = dft_table(N2, True)
    own_halves = masked.reshape(2, channels_dev, frame_count, TAPS)
    previous = jnp.concatenate([tail_in[:, :, None], own_halves[:, :, :-1]], axis=2)
    frames = jnp.concatenate([previous, own_halves], axis=3).reshape(
        2, channels_dev, frame_count, N1, N2
    )
    section_a = jnp.einsum(
        "pkqt,qcfts->cfpks", forward_first, frames, preferred_element_type=jnp.float32
    )
    cos_twist, sin_twist = twist_table(jnp.arange(N1, dtype=jnp.int32), N2)
    real_a = section_a[:, :, 0]
    imag_a = section_a[:, :, 1]
    twisted = jnp.stack(
        [real_a * cos_twist + imag_a * sin_twist, imag_a * cos_twist - real_a * sin_twist], axis=2
    ).astype(jnp.bfloat16)
    spectrum = jnp.einsum(
        "rlps,cfpks->kfcrl", forward_second, twisted, preferred_element_type=jnp.float32
    )
    cos_disp, sin_disp = phase_table(dispersion)
    cos_disp = jnp.swapaxes(cos_disp, 0, 1)[:, None]
    sin_disp = jnp.swapaxes(sin_disp, 0, 1)[:, None]
    real_s = spectrum[:, :, :, 0]
    imag_s = spectrum[:, :, :, 1]
    dispersed = jnp.concatenate(
        [real_s * cos_disp - imag_s * sin_disp, real_s * sin_disp + imag_s * cos_disp], axis=3
    ).astype(jnp.bfloat16)
    by_bins = lax.all_to_all(dispersed, ("tm", "chan"), split_axis=0, concat_axis=0, tiled=True)
    tm_count = lax.axis_size("tm")
    chan_count = lax.axis_size("chan")
    bins_rows = N1 // (tm_count * chan_count)
    grid = by_bins.reshape(tm_count, chan_count, bins_rows, frame_count, channels_dev, 2 * N2)
    columns = jnp.transpose(grid, (0, 3, 1, 4, 2, 5)).reshape(
        tm_count * frame_count, chan_count * channels_dev, bins_rows * 2 * N2
    )
    picks = jnp.broadcast_to(bin_block.T[:, None, :], (bins_rows, 2, N2)).reshape(1, -1)
    equalised = equalise(columns, equaliser, picks)
    equalised = equalised.reshape(
        tm_count, frame_count, chan_count, channels_dev, bins_rows, 2 * N2
    )
    equalised = jnp.transpose(equalised, (0, 2, 4, 1, 3, 5)).reshape(
        N1, frame_count, channels_dev, 2 * N2
    )
    returned = lax.all_to_all(equalised, ("tm", "chan"), split_axis=0, concat_axis=0, tiled=True)
    returned = returned.reshape(N1, frame_count, channels_dev, 2, N2)
    restored = invert_second(returned, jnp.arange(N1, dtype=jnp.int32), inverse_second)
    values = jnp.einsum(
        "rupj,cjfpt->rcfut",
        inverse_first[:, half_rows:],
        restored,
        preferred_element_type=jnp.float32,
    )
    values = values.reshape(2, channels_dev, frame_count * TAPS)
    return (values * channel_mask.astype(jnp.float32)[None, :, None]).astype(jnp.bfloat16)


def solution(mesh):
    in_specs = (
        P(None, "chan", ("groups", "tm", "sub")),
        P("chan"),
        P("chan"),
        P(("tm", "chan"), None, None, None),
        P(None, ("tm", "chan")),
    )
    out_specs = P(None, "chan", ("groups", "tm", "sub"))
    return jax.shard_map(
        on_device, mesh=mesh, in_specs=in_specs, out_specs=out_specs, check_vma=False
    )
```

```python
import functools
import math

import jax
import jax.numpy as jnp
from jax import lax
from jax.experimental import pallas as pl
from jax.experimental.pallas import tpu as pltpu
from jax.sharding import PartitionSpec as P

TAPS = 4096
N1 = 128
NFFT = 8192
N2 = 64


def from_behind(value, axis, by):
    devices = lax.axis_size(axis)
    pairs = [(i, i + by) for i in range(devices) if 0 <= i + by < devices]
    return lax.ppermute(value, axis, pairs)


def dft_table(length, inverse):
    counter = jnp.arange(length, dtype=jnp.int32)
    product = counter[:, None] * counter[None, :] % length
    angle = product.astype(jnp.float32) * (2.0 * math.pi / length)
    factor = 1.0 / math.sqrt(length)
    cosine = jnp.cos(angle) * factor
    sine = jnp.sin(angle) * factor
    if inverse:
        upper = jnp.stack([cosine, -sine], axis=1)
        lower = jnp.stack([sine, cosine], axis=1)
    else:
        upper = jnp.stack([cosine, sine], axis=1)
        lower = jnp.stack([-sine, cosine], axis=1)
    return jnp.stack([upper, lower], axis=0).astype(jnp.bfloat16)


def twist_table(first_rows, columns):
    seconds = jnp.arange(columns, dtype=jnp.int32)
    product = first_rows[:, None] * seconds[None, :] % NFFT
    angle = product.astype(jnp.float32) * (2.0 * math.pi / NFFT)
    return (jnp.cos(angle), jnp.sin(angle))


def phase_table(dispersion):
    first_rows = jnp.arange(N1, dtype=jnp.int32)
    seconds = jnp.arange(N2, dtype=jnp.int32)
    bins = first_rows[:, None] + N1 * seconds[None, :]
    centred = jnp.where(bins < NFFT // 2, bins, bins - NFFT)
    freq_sq = (centred * centred).astype(jnp.float32) / float(NFFT * NFFT)
    quarter = jnp.mod(centred, 4).astype(jnp.float32) * (0.5 * math.pi)
    phase = dispersion[:, None, None] * freq_sq[None] - quarter[None]
    return (jnp.cos(phase), jnp.sin(phase))


def invert_second(spectra, first_rows, inverse_second):
    partial_value = jnp.einsum(
        "rspk,jfcpk->cjfrs", inverse_second, spectra, preferred_element_type=jnp.float32
    )
    cos_inv, sin_inv = twist_table(first_rows, N2)
    cos_inv = cos_inv[:, None, :]
    sin_inv = sin_inv[:, None, :]
    real_g = partial_value[:, :, :, 0]
    imag_g = partial_value[:, :, :, 1]
    turned = jnp.stack(
        [real_g * cos_inv - imag_g * sin_inv, imag_g * cos_inv + real_g * sin_inv], axis=3
    )
    return turned.astype(jnp.bfloat16)


def equalise_kernel(parts, picks_ref, weights_ref, *refs):
    out_ref = refs[parts]
    shares = refs[0].shape[1]
    pieces = [refs[part][0, share] for share in range(shares) for part in range(parts)]
    values = jnp.concatenate([piece.astype(jnp.float32) for piece in pieces], axis=0)
    width = values.shape[1]
    outputs = out_ref.shape[1]
    chosen = jnp.broadcast_to(picks_ref[...], values.shape)
    mixed = jnp.zeros((2 * outputs, width), jnp.float32)
    for block in range(weights_ref.shape[0]):
        part = jnp.where(chosen == block, values, 0.0).astype(jnp.bfloat16)
        mixed = mixed + jnp.dot(
            weights_ref[block], part, preferred_element_type=jnp.float32
        )
    lane = lax.broadcasted_iota(jnp.int32, (outputs, 2 * N2), 1)
    for start in range(0, width, 2 * N2):
        by_real = mixed[:outputs, start : start + 2 * N2]
        by_imag = pltpu.roll(mixed[outputs:, start : start + 2 * N2], N2, 1)
        turned = by_real + jnp.where(lane < N2, -by_imag, by_imag)
        out_ref[0, :, start : start + 2 * N2] = turned.astype(jnp.bfloat16)


def equalise(columns, weights, picks):
    frames, _, _, lanes = columns[0].shape
    blocks, rows, channels = weights.shape
    outputs = rows // 2
    width = math.gcd(lanes, 8 * N2)
    flops = 2 * frames * lanes * blocks * rows * channels
    moved = 2 * (weights.size + frames * lanes * (channels + outputs))
    return pl.pallas_call(
        functools.partial(equalise_kernel, len(columns)),
        grid=(frames, lanes // width),
        in_specs=[
            pl.BlockSpec((1, width), lambda m, i: (0, i)),
            pl.BlockSpec((blocks, rows, channels), lambda m, i: (0, 0, 0)),
        ]
        + [
            pl.BlockSpec((1,) + part.shape[1:3] + (width,), lambda m, i: (m, 0, 0, i))
            for part in columns
        ],
        out_specs=pl.BlockSpec((1, outputs, width), lambda m, i: (m, 0, i)),
        out_shape=jax.ShapeDtypeStruct((frames, outputs, lanes), jnp.bfloat16),
        cost_estimate=pl.CostEstimate(flops=flops, bytes_accessed=moved, transcendentals=0),
        compiler_params=pltpu.CompilerParams(vmem_limit_bytes=40 * 1024 * 1024),
    )(picks, weights, *columns)


def to_bins(signal, channel_mask, dispersion, forward_first, forward_second):
    channels = signal.shape[1]
    frame_count = signal.shape[2] // TAPS
    masked = signal * channel_mask.astype(jnp.bfloat16)[None, :, None]
    tail_in = from_behind(masked[:, :, -TAPS:], ("tm", "sub"), 1)
    own_halves = masked.reshape(2, channels, frame_count, TAPS)
    previous = jnp.concatenate([tail_in[:, :, None], own_halves[:, :, :-1]], axis=2)
    frames = jnp.concatenate([previous, own_halves], axis=3).reshape(
        2, channels, frame_count, N1, N2
    )
    section_a = jnp.einsum(
        "pkqt,qcfts->cfpks", forward_first, frames, preferred_element_type=jnp.float32
    )
    cos_twist, sin_twist = twist_table(jnp.arange(N1, dtype=jnp.int32), N2)
    real_a = section_a[:, :, 0]
    imag_a = section_a[:, :, 1]
    twisted = jnp.stack(
        [real_a * cos_twist + imag_a * sin_twist, imag_a * cos_twist - real_a * sin_twist], axis=2
    ).astype(jnp.bfloat16)
    spectrum = jnp.einsum(
        "rlps,cfpks->kfcrl", forward_second, twisted, preferred_element_type=jnp.float32
    )
    cos_disp, sin_disp = phase_table(dispersion)
    cos_disp = jnp.swapaxes(cos_disp, 0, 1)[:, None]
    sin_disp = jnp.swapaxes(sin_disp, 0, 1)[:, None]
    real_s = spectrum[:, :, :, 0]
    imag_s = spectrum[:, :, :, 1]
    return jnp.concatenate(
        [real_s * cos_disp - imag_s * sin_disp, real_s * sin_disp + imag_s * cos_disp], axis=3
    ).astype(jnp.bfloat16)


def from_bins(returned, channel_mask, inverse_first, inverse_second):
    _, frame_count, channels, _ = returned.shape
    returned = returned.reshape(N1, frame_count, channels, 2, N2)
    restored = invert_second(returned, jnp.arange(N1, dtype=jnp.int32), inverse_second)
    values = jnp.einsum(
        "rupj,cjfpt->rcfut",
        inverse_first[:, N1 // 2 :],
        restored,
        preferred_element_type=jnp.float32,
    )
    values = values.reshape(2, channels, frame_count * TAPS)
    return (values * channel_mask.astype(jnp.float32)[None, :, None]).astype(jnp.bfloat16)


def on_device(signal, channel_mask, dispersion, equaliser, bin_block):
    channels_dev = signal.shape[1]
    frame_count = signal.shape[2] // TAPS
    tm_count = lax.axis_size("tm")
    chan_count = lax.axis_size("chan")
    bins_rows = N1 // (tm_count * chan_count)
    first = -(-channels_dev // 16) * 8
    parts = ((0, first), (first, channels_dev))
    forward = (dft_table(N1, False), dft_table(N2, False))
    inverse = (dft_table(N1, True), dft_table(N2, True))
    columns = []
    for low, high in parts:
        dispersed = to_bins(
            signal[:, low:high], channel_mask[low:high], dispersion[low:high], *forward
        )
        by_bins = lax.all_to_all(
            dispersed, ("tm", "chan"), split_axis=0, concat_axis=0, tiled=True
        )
        grid = by_bins.reshape(tm_count, chan_count, bins_rows, frame_count, high - low, 2 * N2)
        columns.append(
            jnp.transpose(grid, (0, 3, 1, 4, 2, 5)).reshape(
                tm_count * frame_count, chan_count, high - low, bins_rows * 2 * N2
            )
        )
    picks = jnp.broadcast_to(bin_block.T[:, None, :], (bins_rows, 2, N2)).reshape(1, -1)
    blocks, _, _, channels = equaliser.shape
    weights = equaliser.reshape(blocks, 2, chan_count, channels_dev, channels)
    results = []
    for low, high in parts:
        rows = 2 * chan_count * (high - low)
        mine = weights[:, :, :, low:high].reshape(blocks, rows, channels)
        equalised = equalise(columns, mine, picks).reshape(
            tm_count, frame_count, chan_count, high - low, bins_rows, 2 * N2
        )
        equalised = jnp.transpose(equalised, (0, 2, 4, 1, 3, 5)).reshape(
            N1, frame_count, high - low, 2 * N2
        )
        returned = lax.all_to_all(
            equalised, ("tm", "chan"), split_axis=0, concat_axis=0, tiled=True
        )
        results.append(from_bins(returned, channel_mask[low:high], *inverse))
    return jnp.concatenate(results, axis=1)


def solution(mesh):
    in_specs = (
        P(None, "chan", ("groups", "tm", "sub")),
        P("chan"),
        P("chan"),
        P(("tm", "chan"), None, None, None),
        P(None, ("tm", "chan")),
    )
    out_specs = P(None, "chan", ("groups", "tm", "sub"))
    return jax.shard_map(
        on_device, mesh=mesh, in_specs=in_specs, out_specs=out_specs, check_vma=False
    )
```

```python
import functools
import math

import jax
import jax.numpy as jnp
from jax import lax
from jax.experimental import pallas as pl
from jax.experimental.pallas import tpu as pltpu
from jax.sharding import PartitionSpec as P

TAPS = 4096
N1 = 128
NFFT = 8192
N2 = 64


def from_behind(value, axis, by):
    devices = lax.axis_size(axis)
    pairs = [(i, i + by) for i in range(devices) if 0 <= i + by < devices]
    return lax.ppermute(value, axis, pairs)


def dft_table(length, inverse):
    counter = jnp.arange(length, dtype=jnp.int32)
    product = counter[:, None] * counter[None, :] % length
    angle = product.astype(jnp.float32) * (2.0 * math.pi / length)
    factor = 1.0 / math.sqrt(length)
    cosine = jnp.cos(angle) * factor
    sine = jnp.sin(angle) * factor
    if inverse:
        upper = jnp.stack([cosine, -sine], axis=1)
        lower = jnp.stack([sine, cosine], axis=1)
    else:
        upper = jnp.stack([cosine, sine], axis=1)
        lower = jnp.stack([-sine, cosine], axis=1)
    return jnp.stack([upper, lower], axis=0).astype(jnp.bfloat16)


def twist_table(first_rows, columns):
    seconds = jnp.arange(columns, dtype=jnp.int32)
    product = first_rows[:, None] * seconds[None, :] % NFFT
    angle = product.astype(jnp.float32) * (2.0 * math.pi / NFFT)
    return (jnp.cos(angle), jnp.sin(angle))


def phase_table(dispersion):
    first_rows = jnp.arange(N1, dtype=jnp.int32)
    seconds = jnp.arange(N2, dtype=jnp.int32)
    bins = first_rows[:, None] + N1 * seconds[None, :]
    centred = jnp.where(bins < NFFT // 2, bins, bins - NFFT)
    freq_sq = (centred * centred).astype(jnp.float32) / float(NFFT * NFFT)
    quarter = jnp.mod(centred, 4).astype(jnp.float32) * (0.5 * math.pi)
    phase = dispersion[:, None, None] * freq_sq[None] - quarter[None]
    return (jnp.cos(phase), jnp.sin(phase))


def invert_second(spectra, first_rows, inverse_second):
    partial_value = jnp.einsum(
        "rspk,jfcpk->cjfrs", inverse_second, spectra, preferred_element_type=jnp.float32
    )
    cos_inv, sin_inv = twist_table(first_rows, N2)
    cos_inv = cos_inv[:, None, :]
    sin_inv = sin_inv[:, None, :]
    real_g = partial_value[:, :, :, 0]
    imag_g = partial_value[:, :, :, 1]
    turned = jnp.stack(
        [real_g * cos_inv - imag_g * sin_inv, imag_g * cos_inv + real_g * sin_inv], axis=3
    )
    return turned.astype(jnp.bfloat16)


def equalise_kernel(parts, picks_ref, weights_ref, *refs):
    out_ref = refs[parts]
    shares, rows, size, lanes = out_ref.shape
    values = jnp.concatenate(
        [
            jnp.concatenate(
                [
                    refs[part][share, row].astype(jnp.float32)
                    for share in range(shares)
                    for part in range(parts)
                ],
                axis=0,
            )
            for row in range(rows)
        ],
        axis=1,
    )
    width = values.shape[1]
    outputs = shares * size
    chosen = jnp.broadcast_to(picks_ref[...], values.shape)
    mixed = jnp.zeros((2 * outputs, width), jnp.float32)
    for block in range(weights_ref.shape[0]):
        part = jnp.where(chosen == block, values, 0.0).astype(jnp.bfloat16)
        mixed = mixed + jnp.dot(
            weights_ref[block], part, preferred_element_type=jnp.float32
        )
    lane = lax.broadcasted_iota(jnp.int32, (outputs, lanes), 1)
    for row in range(rows):
        by_real = mixed[:outputs, row * lanes : (row + 1) * lanes]
        by_imag = pltpu.roll(mixed[outputs:, row * lanes : (row + 1) * lanes], N2, 1)
        turned = by_real + jnp.where(lane < N2, -by_imag, by_imag)
        for share in range(shares):
            piece = turned[share * size : (share + 1) * size]
            out_ref[share, row] = piece.astype(jnp.bfloat16)


def equalise(columns, weights, picks, size):
    times, shares, rows, frames, _, lanes = columns[0].shape
    blocks, outputs, channels = weights.shape
    step = math.gcd(rows, 4)
    flops = 2 * times * frames * rows * lanes * blocks * outputs * channels
    moved = 2 * (weights.size + times * frames * rows * lanes * (channels + outputs // 2))

    def spec(channels_part):
        return pl.BlockSpec(
            (None, shares, step, None, channels_part, lanes),
            lambda t, f, i: (t, 0, i, f, 0, 0),
        )

    return pl.pallas_call(
        functools.partial(equalise_kernel, len(columns)),
        grid=(times, frames, rows // step),
        in_specs=[
            pl.BlockSpec((1, step * lanes), lambda t, f, i: (0, i)),
            pl.BlockSpec((blocks, outputs, channels), lambda t, f, i: (0, 0, 0)),
        ]
        + [spec(part.shape[4]) for part in columns],
        out_specs=spec(size),
        out_shape=jax.ShapeDtypeStruct(
            (times, shares, rows, frames, size, lanes), jnp.bfloat16
        ),
        cost_estimate=pl.CostEstimate(flops=flops, bytes_accessed=moved, transcendentals=0),
        compiler_params=pltpu.CompilerParams(vmem_limit_bytes=40 * 1024 * 1024),
    )(picks, weights, *columns)


def to_bins(masked, tail_in, dispersion, forward_first, forward_second):
    channels = masked.shape[1]
    frame_count = masked.shape[2] // TAPS
    own_halves = masked.reshape(2, channels, frame_count, TAPS)
    previous = jnp.concatenate([tail_in[:, :, None], own_halves[:, :, :-1]], axis=2)
    frames = jnp.concatenate([previous, own_halves], axis=3).reshape(
        2, channels, frame_count, N1, N2
    )
    section_a = jnp.einsum(
        "pkqt,qcfts->cfpks", forward_first, frames, preferred_element_type=jnp.float32
    )
    cos_twist, sin_twist = twist_table(jnp.arange(N1, dtype=jnp.int32), N2)
    real_a = section_a[:, :, 0]
    imag_a = section_a[:, :, 1]
    twisted = jnp.stack(
        [real_a * cos_twist + imag_a * sin_twist, imag_a * cos_twist - real_a * sin_twist], axis=2
    ).astype(jnp.bfloat16)
    spectrum = jnp.einsum(
        "rlps,cfpks->kfcrl", forward_second, twisted, preferred_element_type=jnp.float32
    )
    cos_disp, sin_disp = phase_table(dispersion)
    cos_disp = jnp.swapaxes(cos_disp, 0, 1)[:, None]
    sin_disp = jnp.swapaxes(sin_disp, 0, 1)[:, None]
    real_s = spectrum[:, :, :, 0]
    imag_s = spectrum[:, :, :, 1]
    return jnp.concatenate(
        [real_s * cos_disp - imag_s * sin_disp, real_s * sin_disp + imag_s * cos_disp], axis=3
    ).astype(jnp.bfloat16)


def from_bins(returned, channel_mask, inverse_first, inverse_second):
    _, frame_count, channels, _ = returned.shape
    returned = returned.reshape(N1, frame_count, channels, 2, N2)
    restored = invert_second(returned, jnp.arange(N1, dtype=jnp.int32), inverse_second)
    values = jnp.einsum(
        "rupj,cjfpt->rcfut",
        inverse_first[:, N1 // 2 :],
        restored,
        preferred_element_type=jnp.float32,
    )
    values = values.reshape(2, channels, frame_count * TAPS)
    return (values * channel_mask.astype(jnp.float32)[None, :, None]).astype(jnp.bfloat16)


def on_device(signal, channel_mask, dispersion, equaliser, bin_block):
    channels_dev = signal.shape[1]
    frame_count = signal.shape[2] // TAPS
    tm_count = lax.axis_size("tm")
    chan_count = lax.axis_size("chan")
    bins_rows = N1 // (tm_count * chan_count)
    first = -(-channels_dev // 16) * 8
    parts = ((0, first), (first, channels_dev))
    forward = (dft_table(N1, False), dft_table(N2, False))
    inverse = (dft_table(N1, True), dft_table(N2, True))
    columns = []
    mask_half = channel_mask.astype(jnp.bfloat16)
    masked = [signal[:, low:high] * mask_half[None, low:high, None] for low, high in parts]
    tails = [from_behind(part[:, :, -TAPS:], ("tm", "sub"), 1) for part in masked]
    for index, (low, high) in enumerate(parts):
        dispersed = to_bins(masked[index], tails[index], dispersion[low:high], *forward)
        dispersed, tails = lax.optimization_barrier((dispersed, tails))
        by_bins = lax.all_to_all(
            dispersed, ("tm", "chan"), split_axis=0, concat_axis=0, tiled=True
        )
        columns.append(
            by_bins.reshape(
                tm_count, chan_count, bins_rows, frame_count, high - low, 2 * N2
            )
        )
    picks = jnp.broadcast_to(bin_block.T[:, None, :], (bins_rows, 2, N2)).reshape(1, -1)
    blocks, _, _, channels = equaliser.shape
    weights = equaliser.reshape(blocks, 2, chan_count, channels_dev, channels)
    results = []
    for low, high in parts:
        rows = 2 * chan_count * (high - low)
        mine = weights[:, :, :, low:high].reshape(blocks, rows, channels)
        equalised = equalise(columns, mine, picks, high - low).reshape(
            N1, frame_count, high - low, 2 * N2
        )
        returned = lax.all_to_all(
            equalised, ("tm", "chan"), split_axis=0, concat_axis=0, tiled=True
        )
        results.append(from_bins(returned, channel_mask[low:high], *inverse))
    return jnp.concatenate(results, axis=1)


def solution(mesh):
    in_specs = (
        P(None, "chan", ("groups", "tm", "sub")),
        P("chan"),
        P("chan"),
        P(("tm", "chan"), None, None, None),
        P(None, ("tm", "chan")),
    )
    out_specs = P(None, "chan", ("groups", "tm", "sub"))
    return jax.shard_map(
        on_device, mesh=mesh, in_specs=in_specs, out_specs=out_specs, check_vma=False
    )
```
